32 devices in a mesh: grp: 2 (over x), seq: 8 (over z, y), head: 2 (over core).
Axes of the slice: x: 2, y: 2, z: 4, core: 2. Of those that a mesh axis runs over, the one named last changes fastest.
Arguments:
- prompt_hidden: bfloat16 [16, 128, 5120], P(('grp', 'seq')), parts along dimension 0, may hold values from -6 to 6
- key_weight: bfloat16 [5120, 512], P('seq', 'head'), may hold values from -0.078125 to 0.078125
- value_weight: bfloat16 [5120, 512], P('seq', 'head'), may hold values from -0.078125 to 0.078125
- queries: bfloat16 [32, 512, 2560], P(('grp', 'seq'), None, 'head'), parts along dimension 0
- resp_keys: bfloat16 [32, 512, 512], P(('grp', 'seq'), None, 'head'), parts along dimension 0
- resp_values: bfloat16 [32, 512, 512], P(('grp', 'seq'), None, 'head'), parts along dimension 0, may hold values from -6 to 6
- out_grad: bfloat16 [32, 512, 2560], P(('grp', 'seq'), None, 'head'), parts along dimension 0, may hold values from -6 to 6
- counts: int32 [16], P('grp'), parts along dimension 0, may hold values from 1 to 8, 16 in all
- slot_of: int32 [32], P('grp'), parts along dimension 0, may hold values from 0 to 15, each once
- owner: int32 [16], P('grp'), parts along dimension 0, may hold values from 0 to 7, each once
Outputs:
- query_grad: bfloat16 [32, 512, 2560], P(('grp', 'seq'), None, 'head'), parts along dimension 0
- resp_key_grad: bfloat16 [32, 512, 512], P(('grp', 'seq'), None, 'head'), parts along dimension 0
- resp_value_grad: bfloat16 [32, 512, 512], P(('grp', 'seq'), None, 'head'), parts along dimension 0
- prompt_grad: bfloat16 [16, 128, 5120], P(('grp', 'seq'), None, 'head'), parts along dimension 0
The draws below stay inside these ranges and needn't reach their ends.
There are 2 independent parts, one for each index of `grp`. The reference program is written for one: setup_inputs(seed, part) draws one part's arguments, and reference() takes and returns one part's arrays. A program takes and returns all parts, laid end to end along the dimension named above; an argument that names none is the same for every part. Nothing has to cross between parts.
Inputs may be any that keep to these rules, and one draw needn't show every extreme that they name: `counts`: every prompt has one response or more; they add up to 16, and the largest is exactly 8. `slot_of`: A permutation: responses are numbered prompt by prompt in the order of counts; slot s is row s of the slot arrays. `owner`: A permutation.
All inputs are finite; a program needn't handle non-finite values.
Results may differ from the reference program's by a relative error of at most 0.012.
Values may be sent and summed in bfloat16 or wider, within the bound.
A program may use at most 128 MiB of HBM per device.

```python
import math
import jax
import jax.numpy as jnp
import numpy as np
from jax import lax

D = 5120
QH = 20
KVH = 4
HD = 128
PLEN = 128
RLEN = 512
PROMPTS = 8
RESPS = 16
MOST = 8


def common_keys(key):
    return jnp.clip(jax.random.normal(key, (RESPS, RLEN, KVH * HD), jnp.float32), -6.0, 6.0)


def draw_resp_keys(key, part):
    shared = common_keys(key)
    return shared.astype(jnp.bfloat16)


def draw_queries(key, part):
    key = jax.random.fold_in(key, 5)
    base = jnp.clip(jax.random.normal(key, (RESPS, RLEN, QH * HD), jnp.float32), -6.0, 6.0)
    return base.astype(jnp.bfloat16)


def block_levels(stream_key, dims, pieces, smallest, top_value):
    def one(axis_at, parts):
        steps = jax.random.uniform(jax.random.fold_in(jax.random.fold_in(stream_key, 6), axis_at), (parts,), jnp.float32, smallest / len(pieces), top_value / len(pieces))
        return jnp.repeat(jnp.exp(steps), dims[axis_at] // parts).reshape((-1,) + (1,) * (len(dims) - axis_at - 1))

    loudness = one(*pieces[0])
    for cut in pieces[1:]:
        loudness = loudness * one(*cut)
    return loudness


def split_up(amount, total, reach, lean):
    weights = [(1 << 20) // math.isqrt(grade ** lean) + 1 for grade in range(2, amount + 1)]
    surplus, given = total - reach - (amount - 1), [1] * (amount - 1)
    while surplus > 0:
        candidates = [i for i in range(amount - 1) if given[i] < reach]
        mass, remaining = sum([weights[i] for i in candidates]), surplus
        for i in candidates:
            more = min(reach - given[i], max(1, remaining * weights[i] // mass), surplus)
            given[i] = given[i] + more
            surplus = surplus - more
    return np.array([reach] + given)


def uneven(stream_key, amount, total, bound, slope):
    if amount == 2:
        one = jax.random.randint(stream_key, (), max(1, total - bound), min(bound, total - 1) + 1)
        return jnp.stack([one, total - one])
    lengths = jnp.asarray(split_up(amount, total, bound, slope), jnp.int32)
    couples = (amount - 1) // 2
    giver, taker = lengths[1:1 + 2 * couples:2], lengths[2:2 + 2 * couples:2]
    slack = jnp.minimum(giver - 1, bound - taker)
    moved = jax.random.randint(jax.random.fold_in(stream_key, 1), (couples,), 0, 1 << 20) % (slack + 1)
    lengths = lengths.at[1:1 + 2 * couples:2].set(giver - moved).at[2:2 + 2 * couples:2].set(taker + moved)
    return lengths[jax.random.permutation(jax.random.fold_in(stream_key, 2), amount)]


def bell_draw(rng, shape, scale, most, split=(), held_as=jnp.bfloat16):
    loudness = block_levels(rng, shape, split, -0.22, 0.18) if split else 1.0
    entries = jax.random.normal(rng, shape, jnp.float32) * scale * loudness
    return jnp.minimum(jnp.maximum(entries, -most), most).astype(held_as)


def setup_inputs(seed: int = 0, part: int = 0) -> dict:
    splits = jax.random.split(jax.random.key(seed), 11)
    own_keys = jax.random.split(jax.random.fold_in(splits[10], part), 11)
    prompt_hidden = bell_draw(own_keys[0], (PROMPTS, PLEN, D), 1.0, 6.0, ((0, 8),))
    key_weight = bell_draw(splits[1], (D, KVH * HD), D ** -0.5, 0.078125, ((0, 8), (1, 2)))
    value_weight = bell_draw(splits[2], (D, KVH * HD), D ** -0.5, 0.078125, ((0, 8), (1, 2)))
    queries = draw_queries(jax.random.fold_in(jax.random.fold_in(splits[10], part), 71), part)
    resp_keys = draw_resp_keys(jax.random.fold_in(jax.random.fold_in(splits[10], part), 71), part)
    resp_values = bell_draw(own_keys[5], (RESPS, RLEN, KVH * HD), 1.0, 6.0, ((0, 8), (2, 2)))
    out_grad = bell_draw(own_keys[6], (RESPS, RLEN, QH * HD), 1.0, 6.0, ((0, 8), (2, 2)))
    counts = uneven(own_keys[7], PROMPTS, RESPS, MOST, 2).astype(jnp.int32)
    slot_of = jax.random.permutation(own_keys[8], RESPS).astype(jnp.int32)
    owner = jax.random.permutation(own_keys[9], PROMPTS).astype(jnp.int32)
    return {"prompt_hidden": prompt_hidden, "key_weight": key_weight, "value_weight": value_weight, "queries": queries, "resp_keys": resp_keys, "resp_values": resp_values, "out_grad": out_grad, "counts": counts, "slot_of": slot_of, "owner": owner}


def locate(counts, slot_of, owner, first, number):
    wanted = first + jnp.arange(number, dtype=jnp.int32)
    numbers = jnp.arange(slot_of.shape[0], dtype=jnp.int32)
    response = lax.optimization_barrier(jnp.sum(jnp.where(slot_of[None, :] == wanted[:, None], numbers[None, :], 0), axis=1)).astype(jnp.int32)
    ends = jnp.cumsum(counts).astype(jnp.int32)
    prompt = lax.optimization_barrier(jnp.sum((ends[None, :] <= response[:, None]).astype(jnp.int32), axis=1)).astype(jnp.int32)
    blocks = jnp.arange(owner.shape[0], dtype=jnp.int32)
    return lax.optimization_barrier(jnp.sum(jnp.where(blocks[None, :] == prompt[:, None], owner[None, :], 0), axis=1)).astype(jnp.int32)

def attend(query, key, value, grad, plen):
    rows = query.shape[0]
    keys = key.shape[0]
    heads_kv = key.shape[1] // HD
    group = query.shape[1] // (heads_kv * HD)
    scale = 1.0 / math.sqrt(HD)
    query_heads = query.astype(jnp.float32).reshape(rows, heads_kv, group, HD)
    grad_heads = grad.astype(jnp.float32).reshape(rows, heads_kv, group, HD)
    key_heads = key.astype(jnp.float32).reshape(keys, heads_kv, HD)
    value_heads = value.astype(jnp.float32).reshape(keys, heads_kv, HD)
    scores = jnp.einsum('tkgd,ukd->kgtu', query_heads, key_heads) * scale
    visible = jnp.arange(keys)[None, :] - plen <= jnp.arange(rows)[:, None]
    scores = jnp.where(visible, scores, -jnp.inf)
    highest = lax.optimization_barrier(jnp.max(scores, axis=-1, keepdims=True))
    weights = jnp.exp(scores - highest)
    probs = weights / lax.optimization_barrier(jnp.sum(weights, axis=-1, keepdims=True))
    probs_b = probs.astype(jnp.bfloat16).astype(jnp.float32)
    attended = jnp.einsum('kgtu,ukd->tkgd', probs_b, value_heads).astype(jnp.bfloat16).astype(jnp.float32)
    delta = jnp.transpose(lax.optimization_barrier(jnp.sum(grad_heads * attended, axis=-1)), (1, 2, 0))
    dprob = jnp.einsum('tkgd,ukd->kgtu', grad_heads, value_heads)
    dscore = (probs * (dprob - delta[..., None])).astype(jnp.bfloat16).astype(jnp.float32)
    grad_query = (jnp.einsum('kgtu,ukd->tkgd', dscore, key_heads) * scale).astype(jnp.bfloat16)
    grad_key = jnp.einsum('kgtu,tkgd->ukd', dscore, query_heads) * scale
    grad_value = jnp.einsum('kgtu,tkgd->ukd', probs_b, grad_heads)
    return (grad_query.reshape(rows, -1), grad_key.reshape(keys, -1), grad_value.reshape(keys, -1))

def reference(prompt_hidden, key_weight, value_weight, queries, resp_keys, resp_values, out_grad, counts, slot_of, owner):
    flat = prompt_hidden.reshape(PROMPTS * PLEN, D)
    prompt_keys = jnp.dot(flat, key_weight, preferred_element_type=jnp.float32).astype(jnp.bfloat16).reshape(PROMPTS, PLEN, -1)
    prompt_values = jnp.dot(flat, value_weight, preferred_element_type=jnp.float32).astype(jnp.bfloat16).reshape(PROMPTS, PLEN, -1)
    blocks = locate(counts, slot_of, owner, 0, RESPS)

    def one_slot(items):
        query, own_key, own_value, grad, block = items
        key = jnp.concatenate([prompt_keys[block], own_key], axis=0)
        value = jnp.concatenate([prompt_values[block], own_value], axis=0)
        return attend(query, key, value, grad, PLEN)
    grad_query, grad_key, grad_value = lax.map(one_slot, (queries, resp_keys, resp_values, out_grad, blocks))
    width = KVH * HD
    summed_key = jnp.zeros((PROMPTS, PLEN, width), jnp.float32).at[blocks].add(grad_key[:, :PLEN])
    summed_value = jnp.zeros((PROMPTS, PLEN, width), jnp.float32).at[blocks].add(grad_value[:, :PLEN])
    key_rows = summed_key.astype(jnp.bfloat16).reshape(PROMPTS * PLEN, width)
    value_rows = summed_value.astype(jnp.bfloat16).reshape(PROMPTS * PLEN, width)
    prompt_grad = jnp.dot(key_rows, key_weight.T, preferred_element_type=jnp.float32) + jnp.dot(value_rows, value_weight.T, preferred_element_type=jnp.float32)
    prompt_grad = prompt_grad.astype(jnp.bfloat16).reshape(PROMPTS, PLEN, D)
    return (grad_query, grad_key[:, PLEN:].astype(jnp.bfloat16), grad_value[:, PLEN:].astype(jnp.bfloat16), prompt_grad)
```

```python
import functools
import math

import jax
import jax.numpy as jnp
from jax import lax
from jax.experimental import pallas as pl
from jax.experimental.pallas import tpu as pltpu
from jax.sharding import PartitionSpec as P

HD = 128
CHUNK = 256


def locate(counts, slot_of, owner, first, number):
    wanted = first + jnp.arange(number, dtype=jnp.int32)
    numbers = jnp.arange(slot_of.shape[0], dtype=jnp.int32)
    response = jnp.sum(jnp.where(slot_of[None, :] == wanted[:, None], numbers[None, :], 0), axis=1)
    ends = jnp.cumsum(counts)
    prompt = jnp.sum((ends[None, :] <= response[:, None]).astype(jnp.int32), axis=1)
    blocks = jnp.arange(owner.shape[0], dtype=jnp.int32)
    return jnp.sum(jnp.where(blocks[None, :] == prompt[:, None], owner[None, :], 0), axis=1)


def dot(a, b, dims):
    return lax.dot_general(a, b, (dims, ((), ())), preferred_element_type=jnp.float32)


NT = ((1,), (1,))
NN = ((1,), (0,))


def attention_kernel(
    blocks_ref,
    query_ref,
    grad_ref,
    key_ref,
    value_ref,
    prompt_key_ref,
    prompt_value_ref,
    query_grad_ref,
    key_grad_ref,
    value_grad_ref,
    prompt_grad_key_ref,
    prompt_grad_value_ref,
    keys,
    keys_t,
    values,
    acc_key,
    acc_value,
):
    plen = prompt_key_ref.shape[1]
    rows = query_ref.shape[1]
    group = query_ref.shape[2] // HD
    scale = 1.0 / math.sqrt(HD)
    fold = scale * math.log2(math.e)
    keys[:plen, :] = prompt_key_ref[0]
    keys[plen:, :] = key_ref[0]
    values[:plen, :] = prompt_value_ref[0]
    values[plen:, :] = value_ref[0]
    keys_t[...] = keys[...].T
    acc_key[...] = jnp.zeros_like(acc_key)
    acc_value[...] = jnp.zeros_like(acc_value)
    later = lax.broadcasted_iota(jnp.int32, (CHUNK, CHUNK), 0) > lax.broadcasted_iota(
        jnp.int32, (CHUNK, CHUNK), 1
    )
    for part in range(rows // CHUNK):
        low = part * CHUNK
        edge = plen + low
        seen = edge + CHUNK
        for head in range(group):
            lanes = slice(head * HD, (head + 1) * HD)
            query = query_ref[0, low : low + CHUNK, lanes]
            grad = grad_ref[0, low : low + CHUNK, lanes]
            scores = dot(keys[:seen, :], query, NT)
            scores = jnp.concatenate(
                [scores[:edge], jnp.where(later, -jnp.inf, scores[edge:])], axis=0
            )
            highest = jnp.max(scores, axis=0, keepdims=True)
            weights = jnp.exp2((scores - highest) * fold)
            inverse = 1.0 / jnp.sum(weights, axis=0, keepdims=True)
            dprob = dot(values[:seen, :], grad, NT)
            probs = weights * inverse
            delta = jnp.sum(probs * dprob, axis=0, keepdims=True)
            dscore = (probs * (dprob - delta)).astype(jnp.bfloat16)
            acc_value[:seen, :] += dot(probs.astype(jnp.bfloat16), grad, NN)
            acc_key[:seen, :] += dot(dscore, query, NN)
            turned = dot(keys_t[:, :seen], dscore, NN) * scale
            query_grad_ref[0, low : low + CHUNK, lanes] = turned.T.astype(jnp.bfloat16)
    prompt_grad_key_ref[0] = (acc_key[:plen, :] * scale).astype(prompt_grad_key_ref.dtype)
    key_grad_ref[0] = (acc_key[plen:, :] * scale).astype(jnp.bfloat16)
    prompt_grad_value_ref[0] = acc_value[:plen, :].astype(prompt_grad_value_ref.dtype)
    value_grad_ref[0] = acc_value[plen:, :].astype(jnp.bfloat16)


def attention(blocks, queries, out_grad, resp_keys, resp_values, every):
    slots, rows, wide = queries.shape
    heads = resp_keys.shape[2] // HD
    group = wide // heads
    plen = every.shape[1]
    total = plen + rows

    def own(width):
        return pl.BlockSpec((1, rows, width), lambda s, h, b: (s, 0, h))

    small = pl.BlockSpec((1, plen, HD), lambda s, h, b: (s, 0, h))
    spec = pltpu.PrefetchScalarGridSpec(
        num_scalar_prefetch=1,
        grid=(slots, heads),
        in_specs=[
            own(group),
            own(group),
            own(HD),
            own(HD),
            pl.BlockSpec((1, plen, HD), lambda s, h, b: (b[s], 0, h)),
            pl.BlockSpec((1, plen, HD), lambda s, h, b: (b[s], 0, heads + h)),
        ],
        out_specs=[own(group), own(HD), own(HD), small, small],
        scratch_shapes=[
            pltpu.VMEM((total, HD), jnp.bfloat16),
            pltpu.VMEM((HD, total), jnp.bfloat16),
            pltpu.VMEM((total, HD), jnp.bfloat16),
            pltpu.VMEM((total, HD), jnp.float32),
            pltpu.VMEM((total, HD), jnp.float32),
        ],
    )
    shape = jax.ShapeDtypeStruct
    flops = slots * heads * (group // HD) * rows * (plen + rows) * HD * 8
    return pl.pallas_call(
        attention_kernel,
        grid_spec=spec,
        out_shape=[
            shape(queries.shape, jnp.bfloat16),
            shape(resp_keys.shape, jnp.bfloat16),
            shape(resp_keys.shape, jnp.bfloat16),
            shape((slots, plen, heads * HD), jnp.float32),
            shape((slots, plen, heads * HD), jnp.float32),
        ],
        compiler_params=pltpu.CompilerParams(vmem_limit_bytes=48 * 1024 * 1024),
        cost_estimate=pl.CostEstimate(
            flops=flops, bytes_accessed=6 * queries.size, transcendentals=flops // 1024
        ),
    )(blocks, queries, out_grad, resp_keys, resp_values, every, every)


def shards(
    prompt_hidden,
    key_weight,
    value_weight,
    queries,
    resp_keys,
    resp_values,
    out_grad,
    counts,
    slot_of,
    owner,
):
    slots = queries.shape[0]
    prompts = counts.shape[0]
    weight = jnp.concatenate([key_weight, value_weight], axis=1)
    weight_full = lax.all_gather(weight, "seq", axis=0, tiled=True)
    hidden = prompt_hidden[0]
    rows = jnp.dot(hidden, weight_full, preferred_element_type=jnp.float32).astype(jnp.bfloat16)
    first = lax.axis_index("seq") * slots
    blocks = locate(counts, slot_of, owner, first, slots)
    every = lax.all_gather(rows[None], "seq", axis=0, tiled=True)
    grad_query, grad_key, grad_value, prompt_key, prompt_value = attention(
        blocks, queries, out_grad, resp_keys, resp_values, every
    )
    both = jnp.concatenate([prompt_key, prompt_value], axis=2)
    hits = blocks[:, None] == jnp.arange(prompts, dtype=jnp.int32)[None, :]
    terms = jnp.sum(jnp.where(hits[:, :, None, None], both[:, None], 0.0), axis=0)
    moved = lax.all_to_all(terms.astype(jnp.bfloat16), "seq", 0, 0, tiled=True)
    back = jnp.sum(moved.astype(jnp.float32), axis=0).astype(jnp.bfloat16)
    partial_grad = jnp.einsum("lc,dc->ld", back, weight_full, preferred_element_type=jnp.float32)
    prompt_grad = lax.psum_scatter(
        partial_grad[None].astype(jnp.bfloat16), "head", scatter_dimension=2, tiled=True
    )
    return (grad_query, grad_key, grad_value, prompt_grad)


def solution(mesh):
    placed = (
        P(("grp", "seq"), None, None),
        P("seq", "head"),
        P("seq", "head"),
        P(("grp", "seq"), None, "head"),
        P(("grp", "seq"), None, "head"),
        P(("grp", "seq"), None, "head"),
        P(("grp", "seq"), None, "head"),
        P("grp"),
        P("grp"),
        P("grp"),
    )
    return jax.shard_map(
        shards,
        mesh=mesh,
        in_specs=placed,
        out_specs=(P(("grp", "seq"), None, "head"),) * 4,
        check_vma=False,
    )
```

```python
import functools
import math

import jax
import jax.numpy as jnp
from jax import lax
from jax.experimental import pallas as pl
from jax.experimental.pallas import tpu as pltpu
from jax.sharding import PartitionSpec as P

HD = 128
CHUNK = 256


def locate(counts, slot_of, owner, first, number):
    wanted = first + jnp.arange(number, dtype=jnp.int32)
    numbers = jnp.arange(slot_of.shape[0], dtype=jnp.int32)
    response = jnp.sum(jnp.where(slot_of[None, :] == wanted[:, None], numbers[None, :], 0), axis=1)
    ends = jnp.cumsum(counts)
    prompt = jnp.sum((ends[None, :] <= response[:, None]).astype(jnp.int32), axis=1)
    blocks = jnp.arange(owner.shape[0], dtype=jnp.int32)
    return jnp.sum(jnp.where(blocks[None, :] == prompt[:, None], owner[None, :], 0), axis=1)


def dot(a, b, dims):
    return lax.dot_general(a, b, (dims, ((), ())), preferred_element_type=jnp.float32)


NT = ((1,), (1,))
NN = ((1,), (0,))


def attention_kernel(
    blocks_ref,
    query_ref,
    grad_ref,
    key_ref,
    value_ref,
    prompt_key_ref,
    prompt_value_ref,
    query_grad_ref,
    key_grad_ref,
    value_grad_ref,
    prompt_grad_key_ref,
    prompt_grad_value_ref,
    keys,
    keys_t,
    values,
    acc_key,
    acc_value,
):
    plen = prompt_key_ref.shape[1]
    rows = query_ref.shape[1]
    group = query_ref.shape[2] // HD
    scale = 1.0 / math.sqrt(HD)
    fold = scale * math.log2(math.e)
    keys[:plen, :] = prompt_key_ref[0]
    keys[plen:, :] = key_ref[0]
    values[:plen, :] = prompt_value_ref[0]
    values[plen:, :] = value_ref[0]
    keys_t[...] = keys[...].T
    acc_key[...] = jnp.zeros_like(acc_key)
    acc_value[...] = jnp.zeros_like(acc_value)
    later = lax.broadcasted_iota(jnp.int32, (CHUNK, CHUNK), 0) > lax.broadcasted_iota(
        jnp.int32, (CHUNK, CHUNK), 1
    )
    for part in range(rows // CHUNK):
        low = part * CHUNK
        edge = plen + low
        seen = edge + CHUNK
        for head in range(group):
            lanes = slice(head * HD, (head + 1) * HD)
            query = query_ref[0, low : low + CHUNK, lanes]
            grad = grad_ref[0, low : low + CHUNK, lanes]
            scores = dot(keys[:seen, :], query, NT)
            scores = jnp.concatenate(
                [scores[:edge], jnp.where(later, -jnp.inf, scores[edge:])], axis=0
            )
            highest = jnp.max(scores, axis=0, keepdims=True)
            weights = jnp.exp2((scores - highest) * fold)
            inverse = 1.0 / jnp.sum(weights, axis=0, keepdims=True)
            dprob = dot(values[:seen, :], grad, NT)
            probs = weights * inverse
            delta = jnp.sum(probs * dprob, axis=0, keepdims=True)
            dscore = (probs * (dprob - delta)).astype(jnp.bfloat16)
            acc_value[:seen, :] += dot(probs.astype(jnp.bfloat16), grad, NN)
            acc_key[:seen, :] += dot(dscore, query, NN)
            turned = dot(keys_t[:, :seen], dscore, NN) * scale
            query_grad_ref[0, low : low + CHUNK, lanes] = turned.T.astype(jnp.bfloat16)
    prompt_grad_key_ref[0] = (acc_key[:plen, :] * scale).astype(prompt_grad_key_ref.dtype)
    key_grad_ref[0] = (acc_key[plen:, :] * scale).astype(jnp.bfloat16)
    prompt_grad_value_ref[0] = acc_value[:plen, :].astype(prompt_grad_value_ref.dtype)
    value_grad_ref[0] = acc_value[plen:, :].astype(jnp.bfloat16)


def attention(blocks, queries, out_grad, resp_keys, resp_values, every):
    slots, rows, wide = queries.shape
    heads = resp_keys.shape[2] // HD
    group = wide // heads
    plen = every.shape[1]
    total = plen + rows

    def own(width):
        return pl.BlockSpec((1, rows, width), lambda s, h, b: (s, 0, h))

    small = pl.BlockSpec((1, plen, HD), lambda s, h, b: (s, 0, h))
    spec = pltpu.PrefetchScalarGridSpec(
        num_scalar_prefetch=1,
        grid=(slots, heads),
        in_specs=[
            own(group),
            own(group),
            own(HD),
            own(HD),
            pl.BlockSpec((1, plen, HD), lambda s, h, b: (b[s], 0, h)),
            pl.BlockSpec((1, plen, HD), lambda s, h, b: (b[s], 0, heads + h)),
        ],
        out_specs=[own(group), own(HD), own(HD), small, small],
        scratch_shapes=[
            pltpu.VMEM((total, HD), jnp.bfloat16),
            pltpu.VMEM((HD, total), jnp.bfloat16),
            pltpu.VMEM((total, HD), jnp.bfloat16),
            pltpu.VMEM((total, HD), jnp.float32),
            pltpu.VMEM((total, HD), jnp.float32),
        ],
    )
    shape = jax.ShapeDtypeStruct
    flops = slots * heads * (group // HD) * rows * (plen + rows) * HD * 8
    return pl.pallas_call(
        attention_kernel,
        grid_spec=spec,
        out_shape=[
            shape(queries.shape, jnp.bfloat16),
            shape(resp_keys.shape, jnp.bfloat16),
            shape(resp_keys.shape, jnp.bfloat16),
            shape((slots, plen, heads * HD), jnp.float32),
            shape((slots, plen, heads * HD), jnp.float32),
        ],
        compiler_params=pltpu.CompilerParams(vmem_limit_bytes=48 * 1024 * 1024),
        cost_estimate=pl.CostEstimate(
            flops=flops, bytes_accessed=6 * queries.size, transcendentals=flops // 1024
        ),
    )(blocks, queries, out_grad, resp_keys, resp_values, every, every)


MESH = pl.DeviceIdType.MESH


def project_kernel(
    count,
    hidden_ref,
    key_weight_ref,
    value_weight_ref,
    every_ref,
    key_full,
    value_full,
    hidden_all,
    total,
    part_out,
    part_in,
    own_sem,
    pair_sem,
    direct_send,
    direct_recv,
    cross_send,
    cross_recv,
    line_send,
    line_recv,
    side_send,
    side_recv,
):
    plen = hidden_ref.shape[2]
    rows, width = key_weight_ref.shape
    half = rows // 2
    grp = lax.axis_index("grp")
    seq = lax.axis_index("seq")
    z, y = lax.div(seq, 2), lax.rem(seq, 2)
    bit = lax.rem(grp, 2)
    across = {"grp": grp + 1 - 2 * bit}
    pair = {"seq": seq + 1 - 2 * y}

    def ahead(k):
        return {"seq": lax.rem(z + k, count) * 2 + y}

    def behind(k):
        return lax.rem(z + count - k, count)

    barrier = pltpu.get_barrier_semaphore()
    for k in range(1, count):
        pl.semaphore_signal(barrier, inc=1, device_id=ahead(k), device_id_type=MESH)
    pl.semaphore_signal(barrier, inc=1, device_id=across, device_id_type=MESH)
    pl.semaphore_signal(barrier, inc=1, device_id=pair, device_id_type=MESH)
    pl.semaphore_wait(barrier, count + 1)

    def remote(source, target, send, recv, device):
        return pltpu.make_async_remote_copy(
            src_ref=source,
            dst_ref=target,
            send_sem=send,
            recv_sem=recv,
            device_id=device,
            device_id_type=MESH,
        )

    mine = pl.ds(pl.multiple_of(bit * half, 16), half)
    theirs = pl.ds(pl.multiple_of((1 - bit) * half, 16), half)
    weights = ((key_weight_ref, key_full), (value_weight_ref, value_full))
    swap = remote(
        hidden_ref.at[1 - y],
        hidden_all.at[:, pl.ds(plen, plen), :],
        pair_sem.at[0],
        pair_sem.at[1],
        pair,
    )
    direct = {}
    for k in range(count - 1, 0, -1):
        for i, (source, target) in enumerate(weights):
            direct[k, i] = remote(
                source.at[mine],
                target.at[z, mine],
                direct_send.at[i, k],
                direct_recv.at[i, k],
                ahead(k),
            )
            direct[k, i].start()
    swap.start()
    locals_ = [
        pltpu.make_async_copy(key_weight_ref, key_full.at[z], own_sem.at[0]),
        pltpu.make_async_copy(value_weight_ref, value_full.at[z], own_sem.at[1]),
        pltpu.make_async_copy(hidden_ref.at[y], hidden_all.at[:, pl.ds(0, plen), :], own_sem.at[2]),
    ]
    for copy in locals_:
        copy.start()
    for copy in locals_:
        copy.wait()
    swap.wait()

    def add(block, first):
        rows_in = hidden_all[block]
        for i, (_, target) in enumerate(weights):
            lanes = slice(i * width, (i + 1) * width)
            term = dot(rows_in, target[block], NN)
            total[:, lanes] = term if first else total[:, lanes] + term

    add(z, True)
    cross = {}
    for k in range(1, count):
        block = behind(k)
        for i, (source, target) in enumerate(weights):
            remote(
                source.at[mine],
                target.at[block, mine],
                direct_send.at[i, k],
                direct_recv.at[i, k],
                ahead(k),
            ).wait_recv()
            cross[k, i] = remote(
                target.at[block, mine],
                target.at[block, mine],
                cross_send.at[i, k],
                cross_recv.at[i, k],
                across,
            )
            cross[k, i].start()
    for k in range(1, count):
        block = behind(k)
        for i, (_, target) in enumerate(weights):
            remote(
                target.at[block, theirs],
                target.at[block, theirs],
                cross_send.at[i, k],
                cross_recv.at[i, k],
                across,
            ).wait_recv()
        add(block, False)
    part_out[...] = total[plen:, :].astype(jnp.bfloat16)
    parts = remote(part_out, part_in, pair_sem.at[2], pair_sem.at[3], pair)
    parts.start()
    parts.wait()
    every_ref[seq] = (total[:plen, :] + part_in[...].astype(jnp.float32)).astype(jnp.bfloat16)
    line, side = {}, {}
    for k in range(1, count):
        line[k] = remote(
            every_ref.at[seq], every_ref.at[seq], line_send.at[k], line_recv.at[k], ahead(k)
        )
        line[k].start()
    for k in range(count):
        block = behind(k) * 2 + y
        if k > 0:
            remote(
                every_ref.at[block],
                every_ref.at[block],
                line_send.at[k],
                line_recv.at[k],
                ahead(k),
            ).wait_recv()
        side[k] = remote(
            every_ref.at[block], every_ref.at[block], side_send.at[k], side_recv.at[k], pair
        )
        side[k].start()
    for k in range(count):
        block = behind(k) * 2 + 1 - y
        remote(
            every_ref.at[block], every_ref.at[block], side_send.at[k], side_recv.at[k], pair
        ).wait_recv()
    for copy in [*direct.values(), *cross.values(), *line.values(), *side.values()]:
        copy.wait_send()


def project(hidden, key_weight, value_weight, members):
    count = members // 2
    plen = hidden.shape[2]
    rows, width = key_weight.shape
    shape = jax.ShapeDtypeStruct
    vmem = pl.BlockSpec(memory_space=pltpu.VMEM)
    dma = pltpu.SemaphoreType.DMA
    return pl.pallas_call(
        functools.partial(project_kernel, count),
        out_shape=[
            shape((members, plen, 2 * width), jnp.bfloat16),
            shape((count, rows, width), jnp.bfloat16),
            shape((count, rows, width), jnp.bfloat16),
        ],
        in_specs=[vmem] * 3,
        out_specs=[vmem] * 3,
        scratch_shapes=[
            pltpu.VMEM((count, 2 * plen, rows), jnp.bfloat16),
            pltpu.VMEM((2 * plen, 2 * width), jnp.float32),
            pltpu.VMEM((plen, 2 * width), jnp.bfloat16),
            pltpu.VMEM((plen, 2 * width), jnp.bfloat16),
            dma((3,)),
            dma((4,)),
            dma((2, count)),
            dma((2, count)),
            dma((2, count)),
            dma((2, count)),
            dma((count,)),
            dma((count,)),
            dma((count,)),
            dma((count,)),
        ],
        compiler_params=pltpu.CompilerParams(
            collective_id=0, has_side_effects=True, vmem_limit_bytes=48 * 1024 * 1024
        ),
    )(hidden, key_weight, value_weight)


def shards(
    members,
    prompt_hidden,
    key_weight,
    value_weight,
    queries,
    resp_keys,
    resp_values,
    out_grad,
    counts,
    slot_of,
    owner,
):
    slots = queries.shape[0]
    prompts = counts.shape[0]
    plen, model = prompt_hidden.shape[1:]
    rows, width = key_weight.shape
    count = members // 2
    hidden = prompt_hidden[0].reshape(plen, count, 2, rows).transpose(2, 1, 0, 3)
    every, key_half, value_half = project(hidden, key_weight, value_weight, members)
    seq = lax.axis_index("seq")
    blocks = locate(counts, slot_of, owner, seq * slots, slots)
    grad_query, grad_key, grad_value, prompt_key, prompt_value = attention(
        blocks, queries, out_grad, resp_keys, resp_values, every
    )
    both = jnp.concatenate([prompt_key, prompt_value], axis=2)
    hits = blocks[:, None] == jnp.arange(prompts, dtype=jnp.int32)[None, :]
    terms = jnp.sum(jnp.where(hits[:, :, None, None], both[:, None], 0.0), axis=0)
    moved = lax.all_to_all(terms.astype(jnp.bfloat16), "seq", 0, 0, tiled=True)
    back = jnp.sum(moved.astype(jnp.float32), axis=0).astype(jnp.bfloat16)
    pairs = [(i, i ^ 1) for i in range(members)]
    back = jnp.concatenate([back, lax.ppermute(back, "seq", pairs)], axis=0)
    partial_grad = jnp.einsum(
        "lc,zdc->zld", back[:, :width], key_half, preferred_element_type=jnp.float32
    ) + jnp.einsum("lc,zdc->zld", back[:, width:], value_half, preferred_element_type=jnp.float32)
    summed = lax.psum_scatter(
        partial_grad.astype(jnp.bfloat16), "head", scatter_dimension=0, tiled=True
    )
    own = summed[:, :plen]
    other = lax.ppermute(summed[:, plen:], "seq", pairs)
    even = lax.rem(seq, 2) == 0
    placed = jnp.stack([jnp.where(even, own, other), jnp.where(even, other, own)])
    prompt_grad = placed.transpose(2, 1, 0, 3).reshape(1, plen, model // 2)
    return (grad_query, grad_key, grad_value, prompt_grad)


def solution(mesh):
    placed = (
        P(("grp", "seq"), None, None),
        P("seq", "head"),
        P("seq", "head"),
        P(("grp", "seq"), None, "head"),
        P(("grp", "seq"), None, "head"),
        P(("grp", "seq"), None, "head"),
        P(("grp", "seq"), None, "head"),
        P("grp"),
        P("grp"),
        P("grp"),
    )
    return jax.shard_map(
        functools.partial(shards, mesh.shape["seq"]),
        mesh=mesh,
        in_specs=placed,
        out_specs=(P(("grp", "seq"), None, "head"),) * 4,
        check_vma=False,
    )
```

```python
import functools
import math

import jax
import jax.numpy as jnp
from jax import lax
from jax.experimental import pallas as pl
from jax.experimental.pallas import tpu as pltpu
from jax.sharding import PartitionSpec as P

HD = 128
CHUNK = 256


def locate(counts, slot_of, owner, first, number):
    wanted = first + jnp.arange(number, dtype=jnp.int32)
    numbers = jnp.arange(slot_of.shape[0], dtype=jnp.int32)
    response = jnp.sum(jnp.where(slot_of[None, :] == wanted[:, None], numbers[None, :], 0), axis=1)
    ends = jnp.cumsum(counts)
    prompt = jnp.sum((ends[None, :] <= response[:, None]).astype(jnp.int32), axis=1)
    blocks = jnp.arange(owner.shape[0], dtype=jnp.int32)
    return jnp.sum(jnp.where(blocks[None, :] == prompt[:, None], owner[None, :], 0), axis=1)


def dot(a, b, dims):
    return lax.dot_general(a, b, (dims, ((), ())), preferred_element_type=jnp.float32)


NT = ((1,), (1,))
NN = ((1,), (0,))


def attention_kernel(
    blocks_ref,
    query_ref,
    grad_ref,
    key_ref,
    value_ref,
    prompt_key_ref,
    prompt_value_ref,
    query_grad_ref,
    key_grad_ref,
    value_grad_ref,
    prompt_grad_key_ref,
    prompt_grad_value_ref,
    keys,
    keys_t,
    values,
    acc_key,
    acc_value,
):
    plen = prompt_key_ref.shape[1]
    rows = query_ref.shape[1]
    group = query_ref.shape[2] // HD
    scale = 1.0 / math.sqrt(HD)
    fold = scale * math.log2(math.e)
    keys[:plen, :] = prompt_key_ref[0]
    keys[plen:, :] = key_ref[0]
    values[:plen, :] = prompt_value_ref[0]
    values[plen:, :] = value_ref[0]
    keys_t[...] = keys[...].T
    acc_key[...] = jnp.zeros_like(acc_key)
    acc_value[...] = jnp.zeros_like(acc_value)
    later = lax.broadcasted_iota(jnp.int32, (CHUNK, CHUNK), 0) > lax.broadcasted_iota(
        jnp.int32, (CHUNK, CHUNK), 1
    )
    for part in range(rows // CHUNK):
        low = part * CHUNK
        edge = plen + low
        seen = edge + CHUNK
        for head in range(group):
            lanes = slice(head * HD, (head + 1) * HD)
            query = query_ref[0, low : low + CHUNK, lanes]
            grad = grad_ref[0, low : low + CHUNK, lanes]
            scores = dot(keys[:seen, :], query, NT)
            scores = jnp.concatenate(
                [scores[:edge], jnp.where(later, -jnp.inf, scores[edge:])], axis=0
            )
            highest = jnp.max(scores, axis=0, keepdims=True)
            weights = jnp.exp2((scores - highest) * fold)
            inverse = 1.0 / jnp.sum(weights, axis=0, keepdims=True)
            dprob = dot(values[:seen, :], grad, NT)
            probs = weights * inverse
            delta = jnp.sum(probs * dprob, axis=0, keepdims=True)
            dscore = (probs * (dprob - delta)).astype(jnp.bfloat16)
            acc_value[:seen, :] += dot(probs.astype(jnp.bfloat16), grad, NN)
            acc_key[:seen, :] += dot(dscore, query, NN)
            turned = dot(keys_t[:, :seen], dscore, NN) * scale
            query_grad_ref[0, low : low + CHUNK, lanes] = turned.T.astype(jnp.bfloat16)
    prompt_grad_key_ref[0] = (acc_key[:plen, :] * scale).astype(prompt_grad_key_ref.dtype)
    key_grad_ref[0] = (acc_key[plen:, :] * scale).astype(jnp.bfloat16)
    prompt_grad_value_ref[0] = acc_value[:plen, :].astype(prompt_grad_value_ref.dtype)
    value_grad_ref[0] = acc_value[plen:, :].astype(jnp.bfloat16)


def attention(blocks, queries, out_grad, resp_keys, resp_values, every):
    slots, rows, wide = queries.shape
    heads = resp_keys.shape[2] // HD
    group = wide // heads
    plen = every.shape[1]
    total = plen + rows

    def own(width):
        return pl.BlockSpec((1, rows, width), lambda s, h, b: (s, 0, h))

    small = pl.BlockSpec((1, plen, HD), lambda s, h, b: (s, 0, h))
    spec = pltpu.PrefetchScalarGridSpec(
        num_scalar_prefetch=1,
        grid=(slots, heads),
        in_specs=[
            own(group),
            own(group),
            own(HD),
            own(HD),
            pl.BlockSpec((1, plen, HD), lambda s, h, b: (b[s], 0, h)),
            pl.BlockSpec((1, plen, HD), lambda s, h, b: (b[s], 0, heads + h)),
        ],
        out_specs=[own(group), own(HD), own(HD), small, small],
        scratch_shapes=[
            pltpu.VMEM((total, HD), jnp.bfloat16),
            pltpu.VMEM((HD, total), jnp.bfloat16),
            pltpu.VMEM((total, HD), jnp.bfloat16),
            pltpu.VMEM((total, HD), jnp.float32),
            pltpu.VMEM((total, HD), jnp.float32),
        ],
    )
    shape = jax.ShapeDtypeStruct
    flops = slots * heads * (group // HD) * rows * (plen + rows) * HD * 8
    return pl.pallas_call(
        attention_kernel,
        grid_spec=spec,
        out_shape=[
            shape(queries.shape, jnp.bfloat16),
            shape(resp_keys.shape, jnp.bfloat16),
            shape(resp_keys.shape, jnp.bfloat16),
            shape((slots, plen, heads * HD), jnp.float32),
            shape((slots, plen, heads * HD), jnp.float32),
        ],
        compiler_params=pltpu.CompilerParams(vmem_limit_bytes=48 * 1024 * 1024),
        cost_estimate=pl.CostEstimate(
            flops=flops, bytes_accessed=6 * queries.size, transcendentals=flops // 1024
        ),
    )(blocks, queries, out_grad, resp_keys, resp_values, every, every)


MESH = pl.DeviceIdType.MESH


def project_kernel(
    count,
    hidden_ref,
    key_weight_ref,
    value_weight_ref,
    every_ref,
    key_full,
    value_full,
    hidden_all,
    total,
    part_out,
    part_in,
    own_sem,
    pair_sem,
    direct_send,
    direct_recv,
    cross_send,
    cross_recv,
    line_send,
    line_recv,
    side_send,
    side_recv,
):
    plen = hidden_ref.shape[2]
    rows, width = key_weight_ref.shape
    half = rows // 2
    grp = lax.axis_index("grp")
    seq = lax.axis_index("seq")
    z, y = lax.div(seq, 2), lax.rem(seq, 2)
    bit = lax.rem(grp, 2)
    across = {"grp": grp + 1 - 2 * bit}
    pair = {"seq": seq + 1 - 2 * y}

    up = {"seq": lax.rem(z + 1, count) * 2 + y}
    down = {"seq": lax.rem(z + count - 1, count) * 2 + y}
    has_up, has_down = z < count - 1, z > 0

    def arrivals(k):
        return (
            (z >= k, lax.rem(z + count - k, count), has_up, up, 0),
            (z + k < count, lax.rem(z + k, count), has_down, down, 1),
        )

    barrier = pltpu.get_barrier_semaphore()
    for k in range(1, count):
        other = {"seq": lax.rem(z + k, count) * 2 + y}
        pl.semaphore_signal(barrier, inc=1, device_id=other, device_id_type=MESH)
    pl.semaphore_signal(barrier, inc=1, device_id=across, device_id_type=MESH)
    pl.semaphore_signal(barrier, inc=1, device_id=pair, device_id_type=MESH)
    pl.semaphore_wait(barrier, count + 1)

    def remote(source, target, send, recv, device):
        return pltpu.make_async_remote_copy(
            src_ref=source,
            dst_ref=target,
            send_sem=send,
            recv_sem=recv,
            device_id=device,
            device_id_type=MESH,
        )

    mine = pl.ds(pl.multiple_of(bit * half, 16), half)
    theirs = pl.ds(pl.multiple_of((1 - bit) * half, 16), half)
    weights = ((key_weight_ref, key_full), (value_weight_ref, value_full))
    swap = remote(
        hidden_ref.at[1 - y],
        hidden_all.at[:, pl.ds(plen, plen), :],
        pair_sem.at[0],
        pair_sem.at[1],
        pair,
    )
    sent = []

    def start(copy, wanted):
        pl.when(wanted)(copy.start)
        sent.append((copy, wanted))

    for i, (source, target) in enumerate(weights):
        for wanted, device, way in ((has_up, up, 0), (has_down, down, 1)):
            copy = remote(
                source.at[mine],
                target.at[z, mine],
                direct_send.at[i, way, 0],
                direct_recv.at[i, z],
                device,
            )
            start(copy, wanted)
    swap.start()
    locals_ = [
        pltpu.make_async_copy(key_weight_ref, key_full.at[z], own_sem.at[0]),
        pltpu.make_async_copy(value_weight_ref, value_full.at[z], own_sem.at[1]),
        pltpu.make_async_copy(hidden_ref.at[y], hidden_all.at[:, pl.ds(0, plen), :], own_sem.at[2]),
    ]
    for copy in locals_:
        copy.start()
    for copy in locals_:
        copy.wait()
    swap.wait()

    def add(block, first):
        rows_in = hidden_all[block]
        for i, (_, target) in enumerate(weights):
            lanes = slice(i * width, (i + 1) * width)
            term = dot(rows_in, target[block], NN)
            total[:, lanes] = term if first else total[:, lanes] + term

    def settle(k):
        for there, block, _, _, _ in arrivals(k):

            @pl.when(there)
            def _():
                for i, (_, target) in enumerate(weights):
                    view = target.at[block, theirs]
                    remote(
                        view, view, cross_send.at[i, block], cross_recv.at[i, block], across
                    ).wait_recv()
                add(block, False)

    add(z, True)
    for k in range(1, count):
        for i, (_, target) in enumerate(weights):
            for there, block, further, device, way in arrivals(k):
                view = target.at[block, mine]
                onward = remote(
                    view, view, direct_send.at[i, way, k], direct_recv.at[i, block], device
                )
                pl.when(there)(onward.wait_recv)
                start(onward, jnp.logical_and(there, further))
                copy = remote(
                    view, view, cross_send.at[i, block], cross_recv.at[i, block], across
                )
                start(copy, there)
        if k > 1:
            settle(k - 1)
    settle(count - 1)
    part_out[...] = total[plen:, :].astype(jnp.bfloat16)
    parts = remote(part_out, part_in, pair_sem.at[2], pair_sem.at[3], pair)
    parts.start()
    parts.wait()
    every_ref[seq] = (total[:plen, :] + part_in[...].astype(jnp.float32)).astype(jnp.bfloat16)
    view = every_ref.at[seq]
    for wanted, device, way in ((has_up, up, 0), (has_down, down, 1)):
        start(remote(view, view, line_send.at[way, 0], line_recv.at[z], device), wanted)
    start(remote(view, view, side_send.at[z], side_recv.at[z], pair), z >= 0)
    for k in range(1, count):
        for there, block, further, device, way in arrivals(k):
            view = every_ref.at[block * 2 + y]
            onward = remote(view, view, line_send.at[way, k], line_recv.at[block], device)
            pl.when(there)(onward.wait_recv)
            start(onward, jnp.logical_and(there, further))
            start(remote(view, view, side_send.at[block], side_recv.at[block], pair), there)
    for block in range(count):
        view = every_ref.at[block * 2 + 1 - y]
        remote(view, view, side_send.at[block], side_recv.at[block], pair).wait_recv()
    for copy, wanted in sent:
        pl.when(wanted)(copy.wait_send)


def project(hidden, key_weight, value_weight, members):
    count = members // 2
    plen = hidden.shape[2]
    rows, width = key_weight.shape
    shape = jax.ShapeDtypeStruct
    vmem = pl.BlockSpec(memory_space=pltpu.VMEM)
    dma = pltpu.SemaphoreType.DMA
    return pl.pallas_call(
        functools.partial(project_kernel, count),
        out_shape=[
            shape((members, plen, 2 * width), jnp.bfloat16),
            shape((count, rows, width), jnp.bfloat16),
            shape((count, rows, width), jnp.bfloat16),
        ],
        in_specs=[vmem] * 3,
        out_specs=[vmem] * 3,
        scratch_shapes=[
            pltpu.VMEM((count, 2 * plen, rows), jnp.bfloat16),
            pltpu.VMEM((2 * plen, 2 * width), jnp.float32),
            pltpu.VMEM((plen, 2 * width), jnp.bfloat16),
            pltpu.VMEM((plen, 2 * width), jnp.bfloat16),
            dma((3,)),
            dma((4,)),
            dma((2, 2, count)),
            dma((2, count)),
            dma((2, count)),
            dma((2, count)),
            dma((2, count)),
            dma((count,)),
            dma((count,)),
            dma((count,)),
        ],
        compiler_params=pltpu.CompilerParams(
            collective_id=0, has_side_effects=True, vmem_limit_bytes=48 * 1024 * 1024
        ),
    )(hidden, key_weight, value_weight)


def shards(
    members,
    prompt_hidden,
    key_weight,
    value_weight,
    queries,
    resp_keys,
    resp_values,
    out_grad,
    counts,
    slot_of,
    owner,
):
    slots = queries.shape[0]
    prompts = counts.shape[0]
    plen, model = prompt_hidden.shape[1:]
    rows, width = key_weight.shape
    count = members // 2
    hidden = prompt_hidden[0].reshape(plen, count, 2, rows).transpose(2, 1, 0, 3)
    every, key_half, value_half = project(hidden, key_weight, value_weight, members)
    seq = lax.axis_index("seq")
    blocks = locate(counts, slot_of, owner, seq * slots, slots)
    grad_query, grad_key, grad_value, prompt_key, prompt_value = attention(
        blocks, queries, out_grad, resp_keys, resp_values, every
    )
    both = jnp.concatenate([prompt_key, prompt_value], axis=2)
    hits = blocks[:, None] == jnp.arange(prompts, dtype=jnp.int32)[None, :]
    terms = jnp.sum(jnp.where(hits[:, :, None, None], both[:, None], 0.0), axis=0)
    moved = lax.all_to_all(terms.astype(jnp.bfloat16), "seq", 0, 0, tiled=True)
    back = jnp.sum(moved.astype(jnp.float32), axis=0).astype(jnp.bfloat16)
    pairs = [(i, i ^ 1) for i in range(members)]
    back = jnp.concatenate([back, lax.ppermute(back, "seq", pairs)], axis=0)
    partial_grad = jnp.einsum(
        "lc,zdc->zld", back[:, :width], key_half, preferred_element_type=jnp.float32
    ) + jnp.einsum("lc,zdc->zld", back[:, width:], value_half, preferred_element_type=jnp.float32)
    summed = lax.psum_scatter(
        partial_grad.astype(jnp.bfloat16), "head", scatter_dimension=0, tiled=True
    )
    own = summed[:, :plen]
    other = lax.ppermute(summed[:, plen:], "seq", pairs)
    even = lax.rem(seq, 2) == 0
    placed = jnp.stack([jnp.where(even, own, other), jnp.where(even, other, own)])
    prompt_grad = placed.transpose(2, 1, 0, 3).reshape(1, plen, model // 2)
    return (grad_query, grad_key, grad_value, prompt_grad)


def solution(mesh):
    placed = (
        P(("grp", "seq"), None, None),
        P("seq", "head"),
        P("seq", "head"),
        P(("grp", "seq"), None, "head"),
        P(("grp", "seq"), None, "head"),
        P(("grp", "seq"), None, "head"),
        P(("grp", "seq"), None, "head"),
        P("grp"),
        P("grp"),
        P("grp"),
    )
    return jax.shard_map(
        functools.partial(shards, mesh.shape["seq"]),
        mesh=mesh,
        in_specs=placed,
        out_specs=(P(("grp", "seq"), None, "head"),) * 4,
        check_vma=False,
    )
```
